32 devices in a mesh: parts: 2 (over x), wide: 16 (over z, y, core).
Axes of the slice: x: 2, y: 2, z: 4, core: 2. Of those that a mesh axis runs over, the one named last changes fastest.
Arguments:
- tokens: bfloat16 [4096, 5120], P(('parts', 'wide')), parts along dimension 0, may hold values from -6 to 6
- key_weight_matrix: bfloat16 [5120, 1024], P('wide'), may hold values from -0.078125 to 0.078125
- key_bias_vector: bfloat16 [1024], replicated, may hold values from -3 to 3
- shrink_factors: bfloat16 [5120, 16384], P(None, ('parts', 'wide')), parts along dimension 1, may hold values from -0.078125 to 0.078125
- expand_factors: bfloat16 [16384, 1024], P(('parts', 'wide')), parts along dimension 0, may hold values from -1.5 to 1.5
- adapter_slot_index: int32 [1024], P('parts'), parts along dimension 0, may hold values from 0 to 511, as said below
- row_adapter_index: int32 [4096], P(('parts', 'wide')), parts along dimension 0, may hold values from 0 to 511, as said below
Outputs:
- keys_out: bfloat16 [4096, 1024], P(('parts', 'wide')), parts along dimension 0
The draws below stay inside these ranges and needn't reach their ends.
There are 2 independent parts, one for each index of `parts`. The reference program is written for one: setup_inputs(seed, part) draws one part's arguments, and reference() takes and returns one part's arrays. A program takes and returns all parts, laid end to end along the dimension named above; an argument that names none is the same for every part. Nothing has to cross between parts.
Inputs may be any that keep to these rules, and one draw needn't show every extreme that they name: A permutation: adapter a's factors sit in slot adapter_slot_index[a]; slot s belongs to device s // 32 of wide. `row_adapter_index`: among the rows of one device, at most 16 have adapters whose slots lie on one device of wide; some device of wide receives exactly 16 from every device.
All inputs are finite; a program needn't handle non-finite values.
Results may differ from the reference program's by a relative error of at most 0.0054.
Values may be sent and summed in bfloat16 or wider, within the bound.
No kernel may reach another device: no remote copies, remote signals or barrier semaphores. Data moves between devices by JAX's collectives and lax.ppermute only.
A program may use at most 64 MiB of HBM per device.

```python
import jax
import jax.numpy as jnp
from jax import lax

MODEL_WIDTH = 5120
KEY_WIDTH = 1024
ADAPTER_RANK = 16
ADP_DEV = 32
ROWS_DEV = 128
ADAPTER_TOTAL = 512
ROWS = 2048
CAP = 16


def slot_layout(key):
    return jax.random.permutation(jax.random.fold_in(key, 101), ADAPTER_TOTAL).astype(jnp.int32)


def draw_adapter_slot_index(key, part):
    placed = slot_layout(key)
    return placed


def draw_row_adapter_index(key, part):
    placed = slot_layout(key)
    key = jax.random.fold_in(key, 2)
    inverse = jnp.zeros((ADAPTER_TOTAL,), jnp.int32).at[placed].set(jnp.arange(ADAPTER_TOTAL, dtype=jnp.int32))
    slot_keepers = ADAPTER_TOTAL // ADP_DEV
    sources = ROWS // ROWS_DEV
    spaces = slot_keepers * CAP
    key_hot, key_level, key_base, key_local, key_order = jax.random.split(key, 5)
    hot = jax.random.randint(key_hot, (), 0, slot_keepers)
    level = jax.random.randint(key_level, (slot_keepers,), 0, 4)
    noise = jax.random.randint(key_base, (sources, spaces), 0, 4096)
    owner = jnp.arange(spaces, dtype=jnp.int32) // CAP
    score = noise + level[owner] * 1024 + jnp.where(owner == hot, 16384, 0)
    score = score * spaces + jnp.arange(spaces, dtype=jnp.int32)
    picks = lax.top_k(score, ROWS_DEV)[1].astype(jnp.int32)
    holder = picks // CAP
    local = jax.random.randint(key_local, (sources, ROWS_DEV), 0, ADP_DEV)
    adapter = inverse[holder * ADP_DEV + local]
    keys_rows = jax.random.split(key_order, sources)
    orders = jax.vmap(lambda k: jax.random.permutation(k, ROWS_DEV))(keys_rows)
    adapter = jnp.take_along_axis(adapter, orders, axis=1)
    return adapter.reshape(ROWS).astype(jnp.int32)


def block_scale(own_key, extent, cuts, least, top_value):
    level = 1.0
    for position, parts in cuts:
        steps = jax.random.uniform(jax.random.fold_in(jax.random.fold_in(own_key, 6), position), (parts,), jnp.float32, least / len(cuts), top_value / len(cuts))
        level = level * jnp.repeat(jnp.exp(steps), extent[position] // parts).reshape((-1,) + (1,) * (len(extent) - 1 - position))
    return level


def normal_values(key, dims, scale, limit, cuts=(), kind=jnp.bfloat16):
    values = jax.random.normal(key, dims, jnp.float32) * scale
    if len(cuts) > 0:
        values = block_scale(key, dims, cuts, -0.22, 0.18) * values
    return jnp.clip(values, min=-limit, max=limit).astype(kind)


def setup_inputs(seed: int = 0, part: int = 0) -> dict:
    streams_of = jax.random.split(jax.random.key(seed), 8)
    part_splits = jax.random.split(jax.random.fold_in(streams_of[7], part), 8)
    return {
        "tokens": normal_values(part_splits[0], (ROWS, MODEL_WIDTH), 1.0, 6.0, ((0, 16),)),
        "key_weight_matrix": normal_values(streams_of[1], (MODEL_WIDTH, KEY_WIDTH), MODEL_WIDTH ** -0.5, 0.078125, ((0, 16),)),
        "key_bias_vector": normal_values(streams_of[2], (KEY_WIDTH,), 0.5, 3.0),
        "shrink_factors": normal_values(part_splits[3], (MODEL_WIDTH, ADAPTER_TOTAL * ADAPTER_RANK), MODEL_WIDTH ** -0.5, 0.078125, ((1, 16),)),
        "expand_factors": normal_values(part_splits[4], (ADAPTER_TOTAL * ADAPTER_RANK, KEY_WIDTH), ADAPTER_RANK ** -0.5, 1.5, ((0, 16),)),
        "adapter_slot_index": draw_adapter_slot_index(jax.random.fold_in(jax.random.fold_in(streams_of[7], part), 71), part),
        "row_adapter_index": draw_row_adapter_index(jax.random.fold_in(jax.random.fold_in(streams_of[7], part), 71), part),
    }


def reference(tokens, key_weight_matrix, key_bias_vector, shrink_factors, expand_factors, adapter_slot_index, row_adapter_index):
    base = jnp.dot(tokens, key_weight_matrix, preferred_element_type=jnp.float32)
    slot = adapter_slot_index[row_adapter_index].astype(jnp.int32)
    shrink_table = shrink_factors.reshape(MODEL_WIDTH, ADAPTER_TOTAL, ADAPTER_RANK)
    expand_table = expand_factors.reshape(ADAPTER_TOTAL, ADAPTER_RANK, KEY_WIDTH)

    def one_block(pair):
        rows_block, slots_block = pair
        picked_a = jnp.take(shrink_table, slots_block, axis=1).astype(jnp.float32)
        shrink_output = jnp.einsum("rd,drk->rk", rows_block.astype(jnp.float32), picked_a).astype(jnp.bfloat16)
        picked_b = jnp.take(expand_table, slots_block, axis=0).astype(jnp.float32)
        return jnp.einsum("rk,rke->re", shrink_output.astype(jnp.float32), picked_b).astype(jnp.bfloat16)

    deltas = lax.map(one_block, (tokens.reshape(ROWS // ROWS_DEV, ROWS_DEV, MODEL_WIDTH), slot.reshape(ROWS // ROWS_DEV, ROWS_DEV)))
    deltas = deltas.reshape(ROWS, KEY_WIDTH)
    total = base + key_bias_vector.astype(jnp.float32) + 2.0 * deltas.astype(jnp.float32)
    return total.astype(jnp.bfloat16)
```

```python
import functools

import jax
import jax.numpy as jnp
from jax import lax
from jax.experimental import pallas as pl
from jax.experimental.pallas import tpu as pltpu
from jax.sharding import PartitionSpec as P

ADAPTER_RANK = 16
LANES = 128
VMEM_LIMIT = 48 * 1024 * 1024
F32 = jnp.float32
BF16 = jnp.bfloat16


def _row_places(slot_ref, adapter_ref, adapters_held, capacity):
    adapters = slot_ref.shape[1]
    rows = adapter_ref.shape[1]
    held_bits = adapters_held.bit_length() - 1
    slots = slot_ref[...]
    high = jnp.broadcast_to((slots >> 6).astype(F32).astype(BF16), (8, adapters))
    low = jnp.broadcast_to((slots & 63).astype(F32).astype(BF16), (8, adapters))
    picks = lax.broadcasted_iota(jnp.int32, (adapters, rows), 0) == adapter_ref[...]
    picks = picks.astype(F32).astype(BF16)
    slot_high = jnp.dot(high, picks, preferred_element_type=F32)
    slot_low = jnp.dot(low, picks, preferred_element_type=F32)
    slot = (slot_high * 64.0 + slot_low)[:1].astype(jnp.int32)
    holder = slot >> held_bits
    local = slot & (adapters_held - 1)
    across = jnp.broadcast_to(holder.astype(F32), (rows, rows))
    earlier = lax.broadcasted_iota(jnp.int32, (rows, rows), 0) < lax.broadcasted_iota(
        jnp.int32, (rows, rows), 1
    )
    same = jnp.where(earlier & (across.T == across), 1.0, 0.0)
    rank = jnp.sum(same, axis=0, keepdims=True).astype(jnp.int32)
    return holder * capacity + rank, local


def _pack_kernel(adapters_held, capacity, slot_ref, adapter_ref, tokens_ref, out_ref, place_ref):
    rows, width = tokens_ref.shape
    places = out_ref.shape[0]
    place, local = _row_places(slot_ref, adapter_ref, adapters_held, capacity)
    place_ref[...] = jnp.broadcast_to(place, place_ref.shape)
    sits = lax.broadcasted_iota(jnp.int32, (places, rows), 0) == place
    labels = jnp.sum(
        jnp.where(sits, (local + 1).astype(F32), 0.0), axis=1, keepdims=True
    )
    chosen = sits.astype(F32).astype(BF16)
    step = 1024 if width % 1024 == 0 else width
    for start in range(0, width, step):
        out_ref[:, start : start + step] = jnp.dot(
            chosen, tokens_ref[:, start : start + step], preferred_element_type=F32
        ).astype(BF16)
    out_ref[:, width:] = jnp.broadcast_to(labels, (places, LANES)).astype(BF16)


def pack(slots, adapters, tokens, adapters_held, capacity, places):
    rows, width = tokens.shape
    return pl.pallas_call(
        functools.partial(_pack_kernel, adapters_held, capacity),
        out_shape=(
            jax.ShapeDtypeStruct((places, width + LANES), BF16),
            jax.ShapeDtypeStruct((8, rows), jnp.int32),
        ),
        compiler_params=pltpu.CompilerParams(vmem_limit_bytes=VMEM_LIMIT),
        cost_estimate=pl.CostEstimate(
            flops=2 * places * rows * width,
            bytes_accessed=2 * (rows + places) * width,
            transcendentals=0,
        ),
        name="pack_rows",
    )(slots, adapters, tokens)


def _adapter_kernel(rows_ref, label_ref, shrink_ref, expand_ref, out_ref, total_ref):
    step = pl.program_id(0)

    @pl.when(step == 0)
    def _():
        total_ref[...] = jnp.zeros_like(total_ref)

    total_ref[...] += jnp.dot(rows_ref[...], shrink_ref[...], preferred_element_type=F32)

    @pl.when(step == pl.num_programs(0) - 1)
    def _():
        places, ranks = total_ref.shape
        owner = lax.broadcasted_iota(jnp.int32, (places, ranks), 1) // ADAPTER_RANK + 1
        keep = label_ref[:, :1].astype(F32) == owner.astype(F32)
        shrunk = jnp.where(keep, total_ref[...], 0.0).astype(BF16)
        out_ref[...] = jnp.dot(shrunk, expand_ref[...], preferred_element_type=F32).astype(BF16)


def adapter_terms(arrived, shrink, expand):
    places = arrived.shape[0]
    width, ranks = shrink.shape
    columns = expand.shape[1]
    step = 1024
    return pl.pallas_call(
        _adapter_kernel,
        grid=(width // step,),
        in_specs=[
            pl.BlockSpec((places, step), lambda k: (0, k)),
            pl.BlockSpec((places, LANES), lambda k: (0, width // LANES)),
            pl.BlockSpec((step, ranks), lambda k: (k, 0)),
            pl.BlockSpec((ranks, columns), lambda k: (0, 0)),
        ],
        out_specs=pl.BlockSpec((places, columns), lambda k: (0, 0)),
        out_shape=jax.ShapeDtypeStruct((places, columns), BF16),
        scratch_shapes=[pltpu.VMEM((places, ranks), F32)],
        compiler_params=pltpu.CompilerParams(vmem_limit_bytes=VMEM_LIMIT),
        cost_estimate=pl.CostEstimate(
            flops=2 * places * ranks * (width + columns),
            bytes_accessed=2 * (places + ranks) * (width + columns),
            transcendentals=0,
        ),
        name="adapter_terms",
    )(arrived, arrived, shrink, expand)


def swap(x, axis, bit):
    size = lax.axis_size(axis)
    return lax.ppermute(x, axis, [(i, i ^ bit) for i in range(size)])


def gather_weights(weights):
    size = lax.axis_size("wide")
    half = weights.shape[0] // 2
    mine = lax.axis_index("parts") * half
    current = lax.dynamic_slice_in_dim(weights, mine, half, 0)
    marks = [(0, 0)]

    def grow(x, known, axis, bit):
        wide, parts = (bit, 0) if axis == "wide" else (0, bit)
        return (
            jnp.concatenate([x, swap(x, axis, bit)], axis=0),
            known + [(w ^ wide, p ^ parts) for w, p in known],
        )

    bit = size // 2
    while bit > 2:
        current, marks = grow(current, marks, "wide", bit)
        bit //= 2
    middle, cut = len(marks) // 2, current.shape[0] // 2
    pieces = []
    for x, known, order in (
        (current[:cut], marks[:middle], (("wide", 2), ("parts", 1))),
        (current[cut:], marks[middle:], (("parts", 1), ("wide", 2))),
    ):
        x, known = grow(x, known, *order[0])
        other, (axis, b) = swap(x, *order[1]), order[1]
        wide, parts = (b, 0) if axis == "wide" else (0, b)
        pieces += [(x, known), (other, [(w ^ wide, p ^ parts) for w, p in known])]
    pieces += [(swap(x, "wide", 1), [(w ^ 1, p) for w, p in known]) for x, known in pieces]
    return pieces


def _base_kernel(marks, me_ref, *refs):
    count = len(marks)
    pieces, tokens_ref, out_ref, held_ref = refs[:count], refs[count], refs[count + 1], refs[count + 2]
    wide, parts = me_ref[0], me_ref[1]
    rows = held_ref.shape[1]
    for piece, known in zip(pieces, marks, strict=True):
        for i, (w, p) in enumerate(known):
            place = (wide ^ w) * 2 + (parts ^ p)
            held_ref[place] = piece[i * rows : (i + 1) * rows, :]
    width, columns = tokens_ref.shape[1], out_ref.shape[1]
    together = 4
    depth = together * rows
    out_ref[...] = jnp.zeros_like(out_ref)

    @pl.loop(0, width // depth)
    def _(k):
        block = held_ref[pl.ds(k * together, together)].reshape(depth, columns)
        left = tokens_ref[:, pl.ds(pl.multiple_of(k * depth, LANES), depth)]
        out_ref[...] += jnp.dot(left, block, preferred_element_type=F32)


def base_product(tokens, pieces, rows):
    marks = [known for _, known in pieces]
    columns = pieces[0][0].shape[1]
    width = tokens.shape[1]
    me = jnp.stack([lax.axis_index("wide"), lax.axis_index("parts")]).astype(jnp.int32)
    vmem = pl.BlockSpec(memory_space=pltpu.VMEM)
    return pl.pallas_call(
        functools.partial(_base_kernel, marks),
        in_specs=[pl.BlockSpec(memory_space=pltpu.SMEM)] + [vmem] * (len(pieces) + 1),
        out_specs=vmem,
        out_shape=jax.ShapeDtypeStruct((tokens.shape[0], columns), F32),
        scratch_shapes=[pltpu.VMEM((width // rows, rows, columns), BF16)],
        compiler_params=pltpu.CompilerParams(vmem_limit_bytes=VMEM_LIMIT),
        cost_estimate=pl.CostEstimate(
            flops=2 * tokens.shape[0] * width * columns,
            bytes_accessed=2 * width * columns,
            transcendentals=0,
        ),
        name="base_product",
    )(me, *[x for x, _ in pieces], tokens)


def _finish_kernel(base_ref, bias_ref, returned_ref, place_ref, out_ref):
    places = returned_ref.shape[0]
    rows = base_ref.shape[0]
    sits = lax.broadcasted_iota(jnp.int32, (places, rows), 0) == place_ref[:1, :]
    chosen = sits.astype(F32).T.astype(BF16)
    terms = jnp.dot(chosen, returned_ref[...], preferred_element_type=F32)
    total = base_ref[...] + bias_ref[...].astype(F32) + 2.0 * terms
    out_ref[...] = total.astype(BF16)


def finish(base, bias, returned, place):
    return pl.pallas_call(
        _finish_kernel,
        out_shape=jax.ShapeDtypeStruct(base.shape, BF16),
        compiler_params=pltpu.CompilerParams(vmem_limit_bytes=VMEM_LIMIT),
        name="add_terms",
    )(base, bias, returned, place)


def per_device(
    tokens,
    key_weight_matrix,
    key_bias_vector,
    shrink_factors,
    expand_factors,
    adapter_slot_index,
    row_adapter_index,
):
    rows, width = tokens.shape
    holders = lax.axis_size("wide")
    capacity = 2 * rows // holders
    places = holders * capacity
    adapters_held = expand_factors.shape[0] // ADAPTER_RANK
    columns = expand_factors.shape[1]

    outgoing, place = pack(
        adapter_slot_index[None, :], row_adapter_index[None, :], tokens, adapters_held, capacity, places
    )
    arrived = lax.all_to_all(
        outgoing.reshape(holders, capacity, width + LANES), "wide", split_axis=0, concat_axis=0, tiled=True
    )
    half = key_weight_matrix.shape[0] // 2
    if half % 16 == 0 and (4 * half) % LANES == 0:
        base = base_product(tokens, gather_weights(key_weight_matrix), half)
    else:
        gathered = lax.all_gather(key_weight_matrix, "wide", axis=0, tiled=True)
        base = jnp.dot(tokens, gathered, preferred_element_type=F32)
    terms = adapter_terms(arrived.reshape(places, width + LANES), shrink_factors, expand_factors)
    returned = lax.all_to_all(
        terms.reshape(holders, capacity, columns), "wide", split_axis=0, concat_axis=0, tiled=True
    )
    return finish(base, key_bias_vector[None, :], returned.reshape(places, columns), place)


def solution(mesh):
    placed = (
        P(("parts", "wide"), None),
        P("wide", None),
        P(),
        P(None, ("parts", "wide")),
        P(("parts", "wide"), None),
        P("parts"),
        P(("parts", "wide")),
    )
    return jax.shard_map(
        per_device,
        mesh=mesh,
        in_specs=placed,
        out_specs=P(("parts", "wide"), None),
        check_vma=False,
    )
```

```python
import functools

import jax
import jax.numpy as jnp
from jax import lax
from jax.experimental import pallas as pl
from jax.experimental.pallas import tpu as pltpu
from jax.sharding import PartitionSpec as P

ADAPTER_RANK = 16
LANES = 128
VMEM_LIMIT = 48 * 1024 * 1024
F32 = jnp.float32
BF16 = jnp.bfloat16


def _row_places(slot_ref, adapter_ref, adapters_held, capacity):
    adapters = slot_ref.shape[1]
    rows = adapter_ref.shape[1]
    held_bits = adapters_held.bit_length() - 1
    slots = slot_ref[...]
    high = jnp.broadcast_to((slots >> 6).astype(F32).astype(BF16), (8, adapters))
    low = jnp.broadcast_to((slots & 63).astype(F32).astype(BF16), (8, adapters))
    picks = lax.broadcasted_iota(jnp.int32, (adapters, rows), 0) == adapter_ref[...]
    picks = picks.astype(F32).astype(BF16)
    slot_high = jnp.dot(high, picks, preferred_element_type=F32)
    slot_low = jnp.dot(low, picks, preferred_element_type=F32)
    slot = (slot_high * 64.0 + slot_low)[:1].astype(jnp.int32)
    holder = slot >> held_bits
    local = slot & (adapters_held - 1)
    across = jnp.broadcast_to(holder.astype(F32), (rows, rows))
    earlier = lax.broadcasted_iota(jnp.int32, (rows, rows), 0) < lax.broadcasted_iota(
        jnp.int32, (rows, rows), 1
    )
    same = jnp.where(earlier & (across.T == across), 1.0, 0.0)
    rank = jnp.sum(same, axis=0, keepdims=True).astype(jnp.int32)
    return holder * capacity + rank, local


def _step(width):
    return 1280 if width % 1280 == 0 else width


def _pack_kernel(adapters_held, capacity, slot_ref, adapter_ref, tokens_ref, out_ref, place_ref):
    rows, width = tokens_ref.shape
    places = out_ref.shape[0]
    place, local = _row_places(slot_ref, adapter_ref, adapters_held, capacity)
    place_ref[...] = jnp.broadcast_to(place, place_ref.shape)
    sits = lax.broadcasted_iota(jnp.int32, (places, rows), 0) == place
    labels = jnp.sum(
        jnp.where(sits, (local + 1).astype(F32), 0.0), axis=1, keepdims=True
    )
    chosen = sits.astype(F32).astype(BF16)
    step = _step(width)
    for start in range(0, width, step):
        out_ref[:, start : start + step] = jnp.dot(
            chosen, tokens_ref[:, start : start + step], preferred_element_type=F32
        ).astype(BF16)
    out_ref[:, width:] = jnp.broadcast_to(labels, (places, LANES)).astype(BF16)


def pack(slots, adapters, tokens, adapters_held, capacity, places):
    rows, width = tokens.shape
    return pl.pallas_call(
        functools.partial(_pack_kernel, adapters_held, capacity),
        out_shape=(
            jax.ShapeDtypeStruct((places, width + LANES), BF16),
            jax.ShapeDtypeStruct((8, rows), jnp.int32),
        ),
        compiler_params=pltpu.CompilerParams(vmem_limit_bytes=VMEM_LIMIT),
        cost_estimate=pl.CostEstimate(
            flops=2 * places * rows * width,
            bytes_accessed=2 * (rows + places) * width,
            transcendentals=0,
        ),
        name="pack_rows",
    )(slots, adapters, tokens)


def _adapter_kernel(rows_ref, label_ref, shrink_ref, expand_ref, out_ref, total_ref):
    step = pl.program_id(0)

    @pl.when(step == 0)
    def _():
        total_ref[...] = jnp.zeros_like(total_ref)

    total_ref[...] += jnp.dot(rows_ref[...], shrink_ref[...], preferred_element_type=F32)

    @pl.when(step == pl.num_programs(0) - 1)
    def _():
        places, ranks = total_ref.shape
        owner = lax.broadcasted_iota(jnp.int32, (places, ranks), 1) // ADAPTER_RANK + 1
        keep = label_ref[:, :1].astype(F32) == owner.astype(F32)
        shrunk = jnp.where(keep, total_ref[...], 0.0).astype(BF16)
        out_ref[...] = jnp.dot(shrunk, expand_ref[...], preferred_element_type=F32).astype(BF16)


def adapter_terms(arrived, shrink, expand):
    places = arrived.shape[0]
    width, ranks = shrink.shape
    columns = expand.shape[1]
    step = 1024
    return pl.pallas_call(
        _adapter_kernel,
        grid=(width // step,),
        in_specs=[
            pl.BlockSpec((places, step), lambda k: (0, k)),
            pl.BlockSpec((places, LANES), lambda k: (0, width // LANES)),
            pl.BlockSpec((step, ranks), lambda k: (k, 0)),
            pl.BlockSpec((ranks, columns), lambda k: (0, 0)),
        ],
        out_specs=pl.BlockSpec((places, columns), lambda k: (0, 0)),
        out_shape=jax.ShapeDtypeStruct((places, columns), BF16),
        scratch_shapes=[pltpu.VMEM((places, ranks), F32)],
        compiler_params=pltpu.CompilerParams(vmem_limit_bytes=VMEM_LIMIT),
        cost_estimate=pl.CostEstimate(
            flops=2 * places * ranks * (width + columns),
            bytes_accessed=2 * (places + ranks) * (width + columns),
            transcendentals=0,
        ),
        name="adapter_terms",
    )(arrived, arrived, shrink, expand)


def swap(x, axis, bit):
    size = lax.axis_size(axis)
    return lax.ppermute(x, axis, [(i, i ^ bit) for i in range(size)])


def gather_weights(weights, size):
    half = weights.shape[0] // 2
    mine = lax.axis_index("parts") * half
    current = lax.dynamic_slice_in_dim(weights, mine, half, 0)
    marks = [(0, 0)]

    def grow(x, known, axis, bit):
        wide, parts = (bit, 0) if axis == "wide" else (0, bit)
        return (
            jnp.concatenate([x, swap(x, axis, bit)], axis=0),
            known + [(w ^ wide, p ^ parts) for w, p in known],
        )

    bit = size // 2
    while bit > 2:
        current, marks = grow(current, marks, "wide", bit)
        bit //= 2
    middle, cut = len(marks) // 2, current.shape[0] // 2
    pieces = []
    for x, known, order in (
        (current[:cut], marks[:middle], (("wide", 2), ("parts", 1))),
        (current[cut:], marks[middle:], (("parts", 1), ("wide", 2))),
    ):
        x, known = grow(x, known, *order[0])
        other, (axis, b) = swap(x, *order[1]), order[1]
        wide, parts = (b, 0) if axis == "wide" else (0, b)
        pieces += [(x, known), (other, [(w ^ wide, p ^ parts) for w, p in known])]
    pieces += [(swap(x, "wide", 1), [(w ^ 1, p) for w, p in known]) for x, known in pieces]
    return pieces


def _finish_kernel(base_ref, bias_ref, returned_ref, place_ref, out_ref):
    places = returned_ref.shape[0]
    rows = base_ref.shape[0]
    sits = lax.broadcasted_iota(jnp.int32, (places, rows), 0) == place_ref[:1, :]
    chosen = sits.astype(F32).T.astype(BF16)
    terms = jnp.dot(chosen, returned_ref[...], preferred_element_type=F32)
    total = base_ref[...] + bias_ref[...].astype(F32) + 2.0 * terms
    out_ref[...] = total.astype(BF16)


def finish(base, bias, returned, place):
    return pl.pallas_call(
        _finish_kernel,
        out_shape=jax.ShapeDtypeStruct(base.shape, BF16),
        compiler_params=pltpu.CompilerParams(vmem_limit_bytes=VMEM_LIMIT),
        name="add_terms",
    )(base, bias, returned, place)


def _pack_direct_kernel(adapters_held, capacity, me_ref, slot_ref, adapter_ref, tokens_ref, out_ref, place_ref):
    rows, width = tokens_ref.shape
    places = out_ref.shape[0]
    place, _ = _row_places(slot_ref, adapter_ref, adapters_held, capacity)
    place_ref[...] = jnp.broadcast_to(place, place_ref.shape)
    sits = lax.broadcasted_iota(jnp.int32, (places, rows), 0) == place
    chosen = sits.astype(F32).astype(BF16)
    step = _step(width)
    for start in range(0, width, step):
        out_ref[:, start : start + step] = jnp.dot(
            chosen, tokens_ref[:, start : start + step], preferred_element_type=F32
        ).astype(BF16)


def pack_direct(half_index, slots, adapters, tokens, adapters_held, capacity, places):
    rows, width = tokens.shape[0], tokens.shape[1] // 2
    adapters_all = slots.shape[1]
    return pl.pallas_call(
        functools.partial(_pack_direct_kernel, adapters_held, capacity),
        grid_spec=pltpu.PrefetchScalarGridSpec(
            num_scalar_prefetch=1,
            grid=(1,),
            in_specs=[
                pl.BlockSpec((1, adapters_all), lambda i, me: (0, 0)),
                pl.BlockSpec((1, rows), lambda i, me: (0, 0)),
                pl.BlockSpec((rows, width), lambda i, me: (0, me[0])),
            ],
            out_specs=[
                pl.BlockSpec((places, width), lambda i, me: (0, 0)),
                pl.BlockSpec((8, rows), lambda i, me: (0, 0)),
            ],
        ),
        out_shape=(
            jax.ShapeDtypeStruct((places, width), BF16),
            jax.ShapeDtypeStruct((8, rows), jnp.int32),
        ),
        compiler_params=pltpu.CompilerParams(vmem_limit_bytes=VMEM_LIMIT),
        cost_estimate=pl.CostEstimate(
            flops=2 * places * rows * width,
            bytes_accessed=2 * (rows + places) * width,
            transcendentals=0,
        ),
        name="pack_direct",
    )(half_index, slots, adapters, tokens)


def _pack_route_kernel(
    adapters_held, capacity, me_ref, slot_ref, own_ref, other_ref, far_ref, came_ref, out_ref
):
    rows, width = far_ref.shape
    places = out_ref.shape[0]
    first = me_ref[0] * (places // 2)
    at = lax.broadcasted_iota(jnp.int32, (places, rows), 0)
    holder = at // (2 * capacity)
    rank = at % (2 * capacity)
    chosen, labels = [], 0.0
    for adapter_ref, shift in ((own_ref, 0), (other_ref, capacity)):
        place, local = _row_places(slot_ref, adapter_ref, adapters_held, capacity)
        here = (rank >= shift) & (rank < shift + capacity)
        sits = here & (first + holder * capacity + rank - shift == place)
        labels += jnp.sum(jnp.where(sits, (local + 1).astype(F32), 0.0), axis=1, keepdims=True)
        chosen.append(sits.astype(F32).astype(BF16))
    step = _step(width)
    for start in range(0, width, step):
        cut = slice(start, start + step)
        out_ref[:, cut] = (
            jnp.dot(chosen[0], far_ref[:, cut], preferred_element_type=F32)
            + jnp.dot(chosen[1], came_ref[:, cut], preferred_element_type=F32)
        ).astype(BF16)
    out_ref[:, width:] = jnp.broadcast_to(labels, (places, LANES)).astype(BF16)


def pack_route(half_index, slots, own, other, far, came, adapters_held, capacity, places):
    rows, width = far.shape
    vmem = pl.BlockSpec(memory_space=pltpu.VMEM)
    return pl.pallas_call(
        functools.partial(_pack_route_kernel, adapters_held, capacity),
        in_specs=[pl.BlockSpec(memory_space=pltpu.SMEM)] + [vmem] * 5,
        out_specs=vmem,
        out_shape=jax.ShapeDtypeStruct((places, width + LANES), BF16),
        compiler_params=pltpu.CompilerParams(vmem_limit_bytes=VMEM_LIMIT),
        cost_estimate=pl.CostEstimate(
            flops=4 * places * rows * width,
            bytes_accessed=2 * (2 * rows + places) * width,
            transcendentals=0,
        ),
        name="pack_route",
    )(half_index, slots, own, other, far, came)


def _split_adapter_kernel(me_ref, direct_ref, routed_ref, shrink_ref, expand_ref, out_ref):
    senders, capacity, width = direct_ref.shape
    ranks = expand_ref.shape[0]
    half = senders // 2
    me = me_ref[0]
    rows = half * capacity
    for mirror in (0, 1):
        block = me if mirror == 0 else 1 - me
        direct = direct_ref[pl.ds(block * half, half)].reshape(rows, width)
        cut = slice(mirror * capacity, (mirror + 1) * capacity)
        routed = routed_ref[:, cut, :width].reshape(rows, width)
        label = routed_ref[:, cut, width:].reshape(rows, LANES)[:, :1].astype(F32)
        at = pl.multiple_of(block * width, LANES)
        past = pl.multiple_of((1 - block) * width, LANES)
        total = jnp.dot(direct, shrink_ref[pl.ds(at, width), :], preferred_element_type=F32)
        total += jnp.dot(routed, shrink_ref[pl.ds(past, width), :], preferred_element_type=F32)
        owner = lax.broadcasted_iota(jnp.int32, (rows, ranks), 1) // ADAPTER_RANK + 1
        shrunk = jnp.where(label == owner.astype(F32), total, 0.0).astype(BF16)
        terms = jnp.dot(shrunk, expand_ref[...], preferred_element_type=F32).astype(BF16)
        out_ref[pl.ds(block * half, half)] = terms.reshape(half, capacity, terms.shape[1])


def split_adapter_terms(half_index, direct, routed, shrink, expand):
    senders, capacity, _ = direct.shape
    places = senders * capacity
    width, ranks = shrink.shape
    columns = expand.shape[1]
    vmem = pl.BlockSpec(memory_space=pltpu.VMEM)
    return pl.pallas_call(
        _split_adapter_kernel,
        in_specs=[pl.BlockSpec(memory_space=pltpu.SMEM)] + [vmem] * 4,
        out_specs=vmem,
        out_shape=jax.ShapeDtypeStruct((senders, capacity, columns), BF16),
        compiler_params=pltpu.CompilerParams(vmem_limit_bytes=VMEM_LIMIT),
        cost_estimate=pl.CostEstimate(
            flops=2 * places * ranks * (width + columns),
            bytes_accessed=2 * (places + ranks) * (width + columns),
            transcendentals=0,
        ),
        name="adapter_terms",
    )(half_index, direct, routed, shrink, expand)


def _half_base_kernel(marks, me_ref, *refs):
    count = len(marks)
    pieces = refs[:count]
    tokens_ref, came_ref, own_ref, other_ref, held_ref, left_ref = refs[count:]
    parts, inside, half_index = me_ref[0], me_ref[1], me_ref[2]
    rows = held_ref.shape[1]
    for piece, known in zip(pieces, marks, strict=True):
        for i, (w, p) in enumerate(known):
            held_ref[(inside ^ w) * 2 + (parts ^ p)] = piece[i * rows : (i + 1) * rows, :]
    own_rows, width = came_ref.shape
    columns = own_ref.shape[1]
    left_ref[:own_rows, :] = tokens_ref[:, pl.ds(pl.multiple_of(half_index * width, LANES), width)]
    left_ref[own_rows:, :] = came_ref[...]
    step = 256 if columns % 256 == 0 else columns

    for start in range(0, columns, step):
        block = held_ref[:, :, start : start + step].reshape(width, step)
        product = jnp.dot(left_ref[...], block, preferred_element_type=F32)
        own_ref[:, start : start + step] = product[:own_rows]
        other_ref[:, start : start + step] = product[own_rows:].astype(BF16)


def half_base_product(me, tokens, came, pieces, rows):
    marks = [known for _, known in pieces]
    columns = pieces[0][0].shape[1]
    own_rows, width = came.shape
    vmem = pl.BlockSpec(memory_space=pltpu.VMEM)
    return pl.pallas_call(
        functools.partial(_half_base_kernel, marks),
        in_specs=[pl.BlockSpec(memory_space=pltpu.SMEM)] + [vmem] * (len(pieces) + 2),
        out_specs=(vmem, vmem),
        out_shape=(
            jax.ShapeDtypeStruct((own_rows, columns), F32),
            jax.ShapeDtypeStruct((own_rows, columns), BF16),
        ),
        scratch_shapes=[
            pltpu.VMEM((width // rows, rows, columns), BF16),
            pltpu.VMEM((2 * own_rows, width), BF16),
        ],
        compiler_params=pltpu.CompilerParams(vmem_limit_bytes=VMEM_LIMIT),
        cost_estimate=pl.CostEstimate(
            flops=4 * own_rows * width * columns,
            bytes_accessed=2 * width * columns,
            transcendentals=0,
        ),
        name="half_base_product",
    )(me, *[x for x, _ in pieces], tokens, came)


def _split_finish_kernel(own_ref, other_ref, bias_ref, returned_ref, place_ref, out_ref):
    places = returned_ref.shape[0]
    rows = own_ref.shape[0]
    sits = lax.broadcasted_iota(jnp.int32, (places, rows), 0) == place_ref[:1, :]
    chosen = sits.astype(F32).T.astype(BF16)
    terms = jnp.dot(chosen, returned_ref[...], preferred_element_type=F32)
    total = own_ref[...] + other_ref[...].astype(F32) + bias_ref[...].astype(F32) + 2.0 * terms
    out_ref[...] = total.astype(BF16)


def split_finish(own, other, bias, returned, place):
    return pl.pallas_call(
        _split_finish_kernel,
        out_shape=jax.ShapeDtypeStruct(own.shape, BF16),
        compiler_params=pltpu.CompilerParams(vmem_limit_bytes=VMEM_LIMIT),
        name="add_terms",
    )(own, other, bias, returned, place)


def split_plan(tokens, weights, bias, shrink, expand, slots, adapters, adapters_held, capacity):
    rows, width = tokens.shape
    holders = lax.axis_size("wide")
    half = holders // 2
    places = holders * capacity
    columns = expand.shape[1]
    wide, parts = lax.axis_index("wide"), lax.axis_index("parts")
    half_index = wide // half
    me = half_index[None].astype(jnp.int32)

    far = lax.dynamic_slice_in_dim(tokens, (1 - half_index) * (width // 2), width // 2, 1)
    came = swap(far, "wide", half)
    other_adapters = swap(adapters, "wide", half)
    outgoing, place = pack_direct(me, slots, adapters, tokens, adapters_held, capacity, places)
    direct = lax.all_to_all(
        outgoing.reshape(holders, capacity, width // 2), "wide", split_axis=0, concat_axis=0, tiled=True
    )
    pieces = gather_weights(weights, half)
    inside = pack_route(me, slots, adapters, other_adapters, far, came, adapters_held, capacity, places)
    groups = [list(range(half)), list(range(half, holders))]
    routed = lax.all_to_all(
        inside.reshape(half, 2 * capacity, width // 2 + LANES),
        "wide",
        split_axis=0,
        concat_axis=0,
        tiled=True,
        axis_index_groups=groups,
    )
    who = jnp.stack([parts, wide % half, half_index]).astype(jnp.int32)
    own, other = half_base_product(who, tokens, came, pieces, weights.shape[0] // 2)
    other = swap(other, "wide", half)
    terms = split_adapter_terms(me, direct, routed, shrink, expand)
    returned = lax.all_to_all(terms, "wide", split_axis=0, concat_axis=0, tiled=True)
    return split_finish(own, other, bias, returned.reshape(places, columns), place)


def per_device(
    tokens,
    key_weight_matrix,
    key_bias_vector,
    shrink_factors,
    expand_factors,
    adapter_slot_index,
    row_adapter_index,
):
    rows, width = tokens.shape
    holders = lax.axis_size("wide")
    capacity = 2 * rows // holders
    places = holders * capacity
    adapters_held = expand_factors.shape[0] // ADAPTER_RANK
    columns = expand_factors.shape[1]

    slots, adapters, bias = adapter_slot_index[None, :], row_adapter_index[None, :], key_bias_vector[None, :]
    half = key_weight_matrix.shape[0] // 2
    if holders >= 8 and capacity % 16 == 0 and half % 16 == 0 and width % (2 * LANES) == 0:
        return split_plan(
            tokens, key_weight_matrix, bias, shrink_factors, expand_factors, slots, adapters, adapters_held, capacity
        )
    outgoing, place = pack(slots, adapters, tokens, adapters_held, capacity, places)
    arrived = lax.all_to_all(
        outgoing.reshape(holders, capacity, width + LANES), "wide", split_axis=0, concat_axis=0, tiled=True
    )
    gathered = lax.all_gather(key_weight_matrix, "wide", axis=0, tiled=True)
    base = jnp.dot(tokens, gathered, preferred_element_type=F32)
    terms = adapter_terms(arrived.reshape(places, width + LANES), shrink_factors, expand_factors)
    returned = lax.all_to_all(
        terms.reshape(holders, capacity, columns), "wide", split_axis=0, concat_axis=0, tiled=True
    )
    return finish(base, bias, returned.reshape(places, columns), place)


def solution(mesh):
    placed = (
        P(("parts", "wide"), None),
        P("wide", None),
        P(),
        P(None, ("parts", "wide")),
        P(("parts", "wide"), None),
        P("parts"),
        P(("parts", "wide")),
    )
    return jax.shard_map(
        per_device,
        mesh=mesh,
        in_specs=placed,
        out_specs=P(("parts", "wide"), None),
        check_vma=False,
    )
```

```python
import functools

import jax
import jax.numpy as jnp
from jax import lax
from jax.experimental import pallas as pl
from jax.experimental.pallas import tpu as pltpu
from jax.sharding import PartitionSpec as P

ADAPTER_RANK = 16
LANES = 128
VMEM_LIMIT = 48 * 1024 * 1024
BASE_PRODUCT = 22 * 10**9
BASE_SUM = 20 * 10**9
F32 = jnp.float32
BF16 = jnp.bfloat16


def _in_team(wide, quarter):
    return wide // (2 * quarter) * quarter + wide % quarter


def _from_team(number, team, quarter):
    return number // quarter * (2 * quarter) + team * quarter + number % quarter


def _row_places(slot_ref, adapter_ref, adapters_held, capacity):
    adapters = slot_ref.shape[1]
    rows = adapter_ref.shape[1]
    held_bits = adapters_held.bit_length() - 1
    slots = slot_ref[...]
    high = jnp.broadcast_to((slots >> 6).astype(F32).astype(BF16), (8, adapters))
    low = jnp.broadcast_to((slots & 63).astype(F32).astype(BF16), (8, adapters))
    picks = lax.broadcasted_iota(jnp.int32, (adapters, rows), 0) == adapter_ref[...]
    picks = picks.astype(F32).astype(BF16)
    slot_high = jnp.dot(high, picks, preferred_element_type=F32)
    slot_low = jnp.dot(low, picks, preferred_element_type=F32)
    slot = (slot_high * 64.0 + slot_low)[:1].astype(jnp.int32)
    holder = slot >> held_bits
    local = slot & (adapters_held - 1)
    across = jnp.broadcast_to(holder.astype(F32), (rows, rows))
    earlier = lax.broadcasted_iota(jnp.int32, (rows, rows), 0) < lax.broadcasted_iota(
        jnp.int32, (rows, rows), 1
    )
    same = jnp.where(earlier & (across.T == across), 1.0, 0.0)
    rank = jnp.sum(same, axis=0, keepdims=True).astype(jnp.int32)
    return holder * capacity + rank, local


def _pack_kernel(adapters_held, capacity, slot_ref, adapter_ref, tokens_ref, out_ref, chosen_ref):
    rows, width = tokens_ref.shape
    places = out_ref.shape[0]
    place, local = _row_places(slot_ref, adapter_ref, adapters_held, capacity)
    sits = lax.broadcasted_iota(jnp.int32, (places, rows), 0) == place
    labels = jnp.sum(
        jnp.where(sits, (local + 1).astype(F32), 0.0), axis=1, keepdims=True
    )
    chosen = sits.astype(F32).astype(BF16)
    chosen_ref[...] = sits.astype(F32).T.astype(BF16)
    step = 1280 if width % 1280 == 0 else width
    for start in range(0, width, step):
        out_ref[:, start : start + step] = jnp.dot(
            chosen, tokens_ref[:, start : start + step], preferred_element_type=F32
        ).astype(BF16)
    out_ref[:, width:] = jnp.broadcast_to(labels, (places, LANES)).astype(BF16)


def pack(slots, adapters, tokens, adapters_held, capacity, places):
    rows, width = tokens.shape
    return pl.pallas_call(
        functools.partial(_pack_kernel, adapters_held, capacity),
        out_shape=(
            jax.ShapeDtypeStruct((places, width + LANES), BF16),
            jax.ShapeDtypeStruct((rows, places), BF16),
        ),
        compiler_params=pltpu.CompilerParams(vmem_limit_bytes=VMEM_LIMIT),
        cost_estimate=pl.CostEstimate(
            flops=2 * places * rows * width,
            bytes_accessed=2 * (rows + places) * width,
            transcendentals=0,
        ),
        name="pack_rows",
    )(slots, adapters, tokens)


def _adapter_kernel(rows_ref, shrink_ref, expand_ref, out_ref):
    places, ranks = rows_ref.shape[0], expand_ref.shape[0]
    width = shrink_ref.shape[0]
    total = jnp.dot(rows_ref[:, :width], shrink_ref[...], preferred_element_type=F32)
    owner = lax.broadcasted_iota(jnp.int32, (places, ranks), 1) // ADAPTER_RANK + 1
    keep = rows_ref[:, width : width + 1].astype(F32) == owner.astype(F32)
    shrunk = jnp.where(keep, total, 0.0).astype(BF16)
    out_ref[...] = jnp.dot(shrunk, expand_ref[...], preferred_element_type=F32).astype(BF16)


def adapter_terms(arrived, shrink, expand):
    places = arrived.shape[0]
    width, ranks = shrink.shape
    columns = expand.shape[1]
    return pl.pallas_call(
        _adapter_kernel,
        out_shape=jax.ShapeDtypeStruct((places, columns), BF16),
        compiler_params=pltpu.CompilerParams(vmem_limit_bytes=VMEM_LIMIT),
        cost_estimate=pl.CostEstimate(
            flops=2 * places * ranks * (width + columns),
            bytes_accessed=2 * (places + ranks) * (width + columns),
            transcendentals=0,
        ),
        name="adapter_terms",
    )(arrived, shrink, expand)


def swap(x, axis, bit):
    size = lax.axis_size(axis)
    return lax.ppermute(x, axis, [(i, i ^ bit) for i in range(size)])


def gather_weights(weights, quarter, came):
    half = weights.shape[0] // 2
    mine = lax.axis_index("parts") * half
    current = lax.dynamic_slice_in_dim(weights, mine, half, 0)
    marks = [(0, 0)]

    def grow(x, known, axis, bit):
        number, parts = (bit, 0) if axis == "wide" else (0, bit)
        across = _from_team(bit, 0, quarter) if axis == "wide" else bit
        return (
            jnp.concatenate([x, swap(x, axis, across)], axis=0),
            known + [(w ^ number, p ^ parts) for w, p in known],
        )

    bit = quarter
    while bit > 2:
        current, marks = grow(current, marks, "wide", bit)
        bit //= 2
    current, _ = lax.optimization_barrier((current, came))
    middle, cut = len(marks) // 2, current.shape[0] // 2
    pieces = []
    for x, known, order in (
        (current[:cut], marks[:middle], (("wide", 2), ("parts", 1))),
        (current[cut:], marks[middle:], (("parts", 1), ("wide", 2))),
    ):
        for axis, bit in order:
            x, known = grow(x, known, axis, bit)
        pieces += [(x, known), (swap(x, "wide", 1), [(w ^ 1, p) for w, p in known])]
    return pieces


def _base_kernel(marks, me_ref, *refs):
    count = len(marks)
    pieces = refs[:count]
    tokens_ref, came_ref, own_ref, other_ref, held_ref, left_ref = refs[count:]
    team, inside, parts = me_ref[0], me_ref[1], me_ref[2]
    rows = held_ref.shape[1]
    for piece, known in zip(pieces, marks, strict=True):
        for i, (w, p) in enumerate(known):
            held_ref[(inside ^ w) * 2 + (parts ^ p)] = piece[i * rows : (i + 1) * rows, :]
    own_rows, width = came_ref.shape
    columns = own_ref.shape[1]
    depth = width // 2
    for upper in (0, 1):
        block = pl.ds(pl.multiple_of((2 * upper + team) * depth, LANES), depth)
        left_ref[:own_rows, upper * depth : (upper + 1) * depth] = tokens_ref[:, block]
    left_ref[own_rows:, :] = came_ref[...]
    step = 256 if columns % 256 == 0 else columns

    for start in range(0, columns, step):
        block = held_ref[:, :, start : start + step].reshape(width, step)
        product = jnp.dot(left_ref[...], block, preferred_element_type=F32)
        own_ref[:, start : start + step] = product[:own_rows]
        other_ref[:, start : start + step] = product[own_rows:].astype(BF16)


def base_product(me, tokens, came, pieces, rows):
    marks = [known for _, known in pieces]
    columns = pieces[0][0].shape[1]
    own_rows, width = came.shape
    vmem = pl.BlockSpec(memory_space=pltpu.VMEM)
    return pl.pallas_call(
        functools.partial(_base_kernel, marks),
        in_specs=[pl.BlockSpec(memory_space=pltpu.SMEM)] + [vmem] * (len(pieces) + 2),
        out_specs=(vmem, vmem),
        out_shape=(
            jax.ShapeDtypeStruct((own_rows, columns), F32),
            jax.ShapeDtypeStruct((own_rows, columns), BF16),
        ),
        scratch_shapes=[
            pltpu.VMEM((width // rows, rows, columns), BF16),
            pltpu.VMEM((2 * own_rows, width), BF16),
        ],
        compiler_params=pltpu.CompilerParams(vmem_limit_bytes=VMEM_LIMIT),
        cost_estimate=pl.CostEstimate(
            flops=BASE_PRODUCT,
            bytes_accessed=2 * width * columns,
            transcendentals=0,
        ),
        name="base_product",
    )(me, *[x for x, _ in pieces], tokens, came)


def _base_sum_kernel(own_ref, other_ref, bias_ref, out_ref):
    out_ref[...] = own_ref[...] + other_ref[...].astype(F32) + bias_ref[...].astype(F32)


def base_sum(own, other, bias):
    return pl.pallas_call(
        _base_sum_kernel,
        out_shape=jax.ShapeDtypeStruct(own.shape, F32),
        cost_estimate=pl.CostEstimate(flops=BASE_SUM, bytes_accessed=10 * own.size, transcendentals=0),
        name="base_sum",
    )(own, other, bias)


def _add_terms_kernel(base_ref, returned_ref, chosen_ref, out_ref):
    terms = jnp.dot(chosen_ref[...], returned_ref[...], preferred_element_type=F32)
    out_ref[...] = (base_ref[...] + 2.0 * terms).astype(BF16)


def add_terms(base, returned, chosen):
    return pl.pallas_call(
        _add_terms_kernel,
        out_shape=jax.ShapeDtypeStruct(base.shape, BF16),
        name="add_terms",
    )(base, returned, chosen)


def per_device(
    tokens,
    key_weight_matrix,
    key_bias_vector,
    shrink_factors,
    expand_factors,
    adapter_slot_index,
    row_adapter_index,
):
    rows, width = tokens.shape
    holders = lax.axis_size("wide")
    capacity = 2 * rows // holders
    places = holders * capacity
    adapters_held = expand_factors.shape[0] // ADAPTER_RANK
    columns = expand_factors.shape[1]

    slots, adapters, bias = adapter_slot_index[None, :], row_adapter_index[None, :], key_bias_vector[None, :]
    outgoing, chosen = pack(slots, adapters, tokens, adapters_held, capacity, places)
    arrived = lax.all_to_all(
        outgoing.reshape(holders, capacity, width + LANES), "wide", split_axis=0, concat_axis=0, tiled=True
    )
    half = key_weight_matrix.shape[0] // 2
    if holders >= 8 and half % 16 == 0 and width % (4 * LANES) == 0:
        quarter, depth = holders // 4, width // 4
        wide, parts = lax.axis_index("wide"), lax.axis_index("parts")
        team = wide // quarter % 2
        far = [lax.dynamic_slice_in_dim(tokens, (2 * upper + 1 - team) * depth, depth, 1) for upper in (0, 1)]
        came = swap(jnp.concatenate(far, axis=1), "wide", quarter)
        pieces = gather_weights(key_weight_matrix, quarter, came)
        me = jnp.stack([team, _in_team(wide, quarter), parts]).astype(jnp.int32)
        own, other = base_product(me, tokens, came, pieces, half)
        arrived, other = lax.optimization_barrier((arrived, other))
        base = base_sum(own, swap(other, "wide", quarter), bias)
    else:
        gathered = lax.all_gather(key_weight_matrix, "wide", axis=0, tiled=True)
        base = jnp.dot(tokens, gathered, preferred_element_type=F32) + bias.astype(F32)
    terms = adapter_terms(arrived.reshape(places, width + LANES), shrink_factors, expand_factors)
    returned = lax.all_to_all(
        terms.reshape(holders, capacity, columns), "wide", split_axis=0, concat_axis=0, tiled=True
    )
    return add_terms(base, returned.reshape(places, columns), chosen)


def solution(mesh):
    placed = (
        P(("parts", "wide"), None),
        P("wide", None),
        P(),
        P(None, ("parts", "wide")),
        P(("parts", "wide"), None),
        P("parts"),
        P(("parts", "wide")),
    )
    return jax.shard_map(
        per_device,
        mesh=mesh,
        in_specs=placed,
        out_specs=P(("parts", "wide"), None),
        check_vma=False,
    )
```

```python
import functools

import jax
import jax.numpy as jnp
from jax import lax
from jax.experimental import pallas as pl
from jax.experimental.pallas import tpu as pltpu
from jax.sharding import PartitionSpec as P

ADAPTER_RANK = 16
LANES = 128
MOST_VMEM = 60 * 1024 * 1024
VMEM_LIMIT = 48 * 1024 * 1024
BASE_PRODUCT = 21 * 10**9
BASE_SUM = 20 * 10**9
F32 = jnp.float32
BF16 = jnp.bfloat16


def _in_team(wide, quarter):
    return wide // (2 * quarter) * quarter + wide % quarter


def _from_team(number, team, quarter):
    return number // quarter * (2 * quarter) + team * quarter + number % quarter


def _step(width):
    return 1280 if width % 1280 == 0 else width


def _row_places(slot_ref, adapter_ref, adapters_held, capacity):
    adapters = slot_ref.shape[1]
    rows = adapter_ref.shape[1]
    held_bits = adapters_held.bit_length() - 1
    slots = slot_ref[...]
    high = jnp.broadcast_to((slots >> 6).astype(F32).astype(BF16), (8, adapters))
    low = jnp.broadcast_to((slots & 63).astype(F32).astype(BF16), (8, adapters))
    picks = lax.broadcasted_iota(jnp.int32, (adapters, rows), 0) == adapter_ref[...]
    picks = picks.astype(F32).astype(BF16)
    slot_high = jnp.dot(high, picks, preferred_element_type=F32)
    slot_low = jnp.dot(low, picks, preferred_element_type=F32)
    slot = (slot_high * 64.0 + slot_low)[:1].astype(jnp.int32)
    holder = slot >> held_bits
    local = slot & (adapters_held - 1)
    across = jnp.broadcast_to(holder.astype(F32), (rows, rows))
    earlier = lax.broadcasted_iota(jnp.int32, (rows, rows), 0) < lax.broadcasted_iota(
        jnp.int32, (rows, rows), 1
    )
    same = jnp.where(earlier & (across.T == across), 1.0, 0.0)
    rank = jnp.sum(same, axis=0, keepdims=True).astype(jnp.int32)
    return holder * capacity + rank, local


def _pack_kernel(adapters_held, capacity, slot_ref, adapter_ref, tokens_ref, out_ref, chosen_ref):
    rows, width = tokens_ref.shape
    places = out_ref.shape[0]
    place, local = _row_places(slot_ref, adapter_ref, adapters_held, capacity)
    sits = lax.broadcasted_iota(jnp.int32, (places, rows), 0) == place
    labels = jnp.sum(
        jnp.where(sits, (local + 1).astype(F32), 0.0), axis=1, keepdims=True
    )
    chosen = sits.astype(F32).astype(BF16)
    chosen_ref[...] = sits.astype(F32).T.astype(BF16)
    step = 1280 if width % 1280 == 0 else width
    for start in range(0, width, step):
        out_ref[:, start : start + step] = jnp.dot(
            chosen, tokens_ref[:, start : start + step], preferred_element_type=F32
        ).astype(BF16)
    out_ref[:, width:] = jnp.broadcast_to(labels, (places, LANES)).astype(BF16)


def pack(slots, adapters, tokens, adapters_held, capacity, places):
    rows, width = tokens.shape
    return pl.pallas_call(
        functools.partial(_pack_kernel, adapters_held, capacity),
        out_shape=(
            jax.ShapeDtypeStruct((places, width + LANES), BF16),
            jax.ShapeDtypeStruct((rows, places), BF16),
        ),
        compiler_params=pltpu.CompilerParams(vmem_limit_bytes=VMEM_LIMIT),
        cost_estimate=pl.CostEstimate(
            flops=2 * places * rows * width,
            bytes_accessed=2 * (rows + places) * width,
            transcendentals=0,
        ),
        name="pack_rows",
    )(slots, adapters, tokens)


def _adapter_kernel(
    rows_ref, shrink_ref, expand_ref, out_ref, held_ref, down_ref, up_ref, terms_ref, came_sem, gone_sem
):
    places = held_ref.shape[0]
    width, ranks = down_ref.shape
    step = width // 8
    cuts = [pl.ds(start, step) for start in range(0, width, step)]
    last = pl.ds(width, LANES)
    moves = []
    for cut in cuts:
        moves.append((rows_ref.at[:, cut], held_ref.at[:, cut]))
        moves.append((shrink_ref.at[cut, :], down_ref.at[cut, :]))
    moves += [(rows_ref.at[:, last], held_ref.at[:, last]), (expand_ref, up_ref)]
    coming = [pltpu.make_async_copy(*move, came_sem.at[i]) for i, move in enumerate(moves)]
    for copy in coming:
        copy.start()
    total = jnp.zeros((places, ranks), F32)
    for i, cut in enumerate(cuts):
        coming[2 * i].wait()
        coming[2 * i + 1].wait()
        total += jnp.dot(held_ref[:, cut], down_ref[cut, :], preferred_element_type=F32)
    coming[-2].wait()
    owner = lax.broadcasted_iota(jnp.int32, (places, ranks), 1) // ADAPTER_RANK + 1
    keep = held_ref[:, width : width + 1].astype(F32) == owner.astype(F32)
    shrunk = jnp.where(keep, total, 0.0).astype(BF16)
    coming[-1].wait()
    columns = terms_ref.shape[1]
    step = 512 if columns % 512 == 0 else columns
    going = []
    for i, start in enumerate(range(0, columns, step)):
        cut = pl.ds(start, step)
        terms_ref[:, cut] = jnp.dot(shrunk, up_ref[:, cut], preferred_element_type=F32).astype(BF16)
        going.append(pltpu.make_async_copy(terms_ref.at[:, cut], out_ref.at[:, cut], gone_sem.at[i]))
        going[-1].start()
    for copy in going:
        copy.wait()


def adapter_terms(arrived, shrink, expand):
    places = arrived.shape[0]
    width, ranks = shrink.shape
    columns = expand.shape[1]
    hbm = pl.BlockSpec(memory_space=pl.ANY)
    return pl.pallas_call(
        _adapter_kernel,
        in_specs=[hbm] * 3,
        out_specs=hbm,
        out_shape=jax.ShapeDtypeStruct((places, columns), BF16),
        scratch_shapes=[
            pltpu.VMEM(arrived.shape, BF16),
            pltpu.VMEM(shrink.shape, BF16),
            pltpu.VMEM(expand.shape, BF16),
            pltpu.VMEM((places, columns), BF16),
            pltpu.SemaphoreType.DMA((2 * 8 + 2,)),
            pltpu.SemaphoreType.DMA((pl.cdiv(columns, 512),)),
        ],
        compiler_params=pltpu.CompilerParams(vmem_limit_bytes=60 * 1024 * 1024),
        cost_estimate=pl.CostEstimate(
            flops=2 * places * ranks * (width + columns),
            bytes_accessed=2 * (places + ranks) * (width + columns),
            transcendentals=0,
        ),
        name="adapter_terms",
    )(arrived, shrink, expand)


def swap(x, axis, bit):
    size = lax.axis_size(axis)
    return lax.ppermute(x, axis, [(i, i ^ bit) for i in range(size)])


def gather_weights(weights, quarter, came):
    half = weights.shape[0] // 2
    mine = lax.axis_index("parts") * half
    own = lax.dynamic_slice_in_dim(weights, mine, half, 0)

    def grow(x, known, axis, bit):
        number, parts = (bit, 0) if axis == "wide" else (0, bit)
        across = _from_team(bit, 0, quarter) if axis == "wide" else bit
        return (
            jnp.concatenate([x, swap(x, axis, across)], axis=0),
            known + [(w ^ number, p ^ parts) for w, p in known],
        )

    first = swap(own, "wide", _from_team(quarter, 0, quarter))
    chains = [(own, [(0, 0)]), (first, [(quarter, 0)])]
    bit = quarter // 2
    while bit > 1:
        grown = grow(*chains[0], "wide", bit)
        x, _ = lax.optimization_barrier((chains[1][0], grown[0]))
        chains = [grown, grow(x, chains[1][1], "wide", bit)]
        bit //= 2
    pieces = []
    for x, known in chains:
        x, _ = lax.optimization_barrier((x, came))
        x, known = grow(x, known, "parts", 1)
        came = x
        pieces += [(x, known), (swap(x, "wide", 1), [(w ^ 1, p) for w, p in known])]
    return pieces


def _base_kernel(marks, me_ref, *refs):
    count = len(marks)
    pieces = refs[:count]
    tokens_ref, came_ref, bias_ref, own_ref, other_ref, held_ref, left_ref = refs[count:]
    team, inside, parts = me_ref[0], me_ref[1], me_ref[2]
    rows = held_ref.shape[1]
    for piece, known in zip(pieces, marks, strict=True):
        for i, (w, p) in enumerate(known):
            held_ref[(inside ^ w) * 2 + (parts ^ p)] = piece[i * rows : (i + 1) * rows, :]
    own_rows, width = came_ref.shape
    columns = own_ref.shape[1]
    depth = width // 2
    for upper in (0, 1):
        block = pl.ds(pl.multiple_of((2 * upper + team) * depth, LANES), depth)
        left_ref[:own_rows, upper * depth : (upper + 1) * depth] = tokens_ref[:, block]
    left_ref[own_rows:, :] = came_ref[...]
    step = 256 if columns % 256 == 0 else columns

    for start in range(0, columns, step):
        block = held_ref[:, :, start : start + step].reshape(width, step)
        product = jnp.dot(left_ref[...], block, preferred_element_type=F32)
        own_ref[:, start : start + step] = product[:own_rows] + bias_ref[:, start : start + step].astype(F32)
        other_ref[:, start : start + step] = product[own_rows:].astype(BF16)


def base_product(me, tokens, came, bias, pieces, rows):
    marks = [known for _, known in pieces]
    columns = pieces[0][0].shape[1]
    own_rows, width = came.shape
    vmem = pl.BlockSpec(memory_space=pltpu.VMEM)
    return pl.pallas_call(
        functools.partial(_base_kernel, marks),
        in_specs=[pl.BlockSpec(memory_space=pltpu.SMEM)] + [vmem] * (len(pieces) + 3),
        out_specs=(vmem, vmem),
        out_shape=(
            jax.ShapeDtypeStruct((own_rows, columns), F32),
            jax.ShapeDtypeStruct((own_rows, columns), BF16),
        ),
        scratch_shapes=[
            pltpu.VMEM((width // rows, rows, columns), BF16),
            pltpu.VMEM((2 * own_rows, width), BF16),
        ],
        compiler_params=pltpu.CompilerParams(vmem_limit_bytes=VMEM_LIMIT),
        cost_estimate=pl.CostEstimate(
            flops=BASE_PRODUCT,
            bytes_accessed=2 * width * columns,
            transcendentals=0,
        ),
        name="base_product",
    )(me, *[x for x, _ in pieces], tokens, came, bias)


def _base_sum_kernel(own_ref, other_ref, out_ref):
    out_ref[...] = own_ref[...] + other_ref[...].astype(F32)


def base_sum(own, other):
    return pl.pallas_call(
        _base_sum_kernel,
        out_shape=jax.ShapeDtypeStruct(own.shape, F32),
        compiler_params=pltpu.CompilerParams(vmem_limit_bytes=VMEM_LIMIT),
        cost_estimate=pl.CostEstimate(flops=BASE_SUM, bytes_accessed=10 * own.size, transcendentals=0),
        name="base_sum",
    )(own, other)


def _add_terms_kernel(base_ref, returned_ref, chosen_ref, out_ref):
    terms = jnp.dot(chosen_ref[...], returned_ref[...], preferred_element_type=F32)
    out_ref[...] = (base_ref[...] + 2.0 * terms).astype(BF16)


def add_terms(base, returned, chosen):
    return pl.pallas_call(
        _add_terms_kernel,
        out_shape=jax.ShapeDtypeStruct(base.shape, BF16),
        compiler_params=pltpu.CompilerParams(vmem_limit_bytes=VMEM_LIMIT),
        name="add_terms",
    )(base, returned, chosen)


def per_device(
    tokens,
    key_weight_matrix,
    key_bias_vector,
    shrink_factors,
    expand_factors,
    adapter_slot_index,
    row_adapter_index,
):
    rows, width = tokens.shape
    holders = lax.axis_size("wide")
    capacity = 2 * rows // holders
    places = holders * capacity
    adapters_held = expand_factors.shape[0] // ADAPTER_RANK
    columns = expand_factors.shape[1]

    slots, adapters, bias = adapter_slot_index[None, :], row_adapter_index[None, :], key_bias_vector[None, :]
    outgoing, chosen = pack(slots, adapters, tokens, adapters_held, capacity, places)
    arrived = lax.all_to_all(
        outgoing.reshape(holders, capacity, width + LANES), "wide", split_axis=0, concat_axis=0, tiled=True
    )
    half = key_weight_matrix.shape[0] // 2
    if holders >= 8 and half % 16 == 0 and width % (4 * LANES) == 0:
        quarter, depth = holders // 4, width // 4
        wide, parts = lax.axis_index("wide"), lax.axis_index("parts")
        team = wide // quarter % 2
        far = [lax.dynamic_slice_in_dim(tokens, (2 * upper + 1 - team) * depth, depth, 1) for upper in (0, 1)]
        came = swap(jnp.concatenate(far, axis=1), "wide", quarter)
        pieces = gather_weights(key_weight_matrix, quarter, came)
        me = jnp.stack([team, _in_team(wide, quarter), parts]).astype(jnp.int32)
        own, other = base_product(me, tokens, came, bias, pieces, half)
        arrived, _ = lax.optimization_barrier((arrived, other))
        base = base_sum(own, swap(other, "wide", quarter))
    else:
        gathered = lax.all_gather(key_weight_matrix, "wide", axis=0, tiled=True)
        base = jnp.dot(tokens, gathered, preferred_element_type=F32) + bias.astype(F32)
    terms = adapter_terms(arrived.reshape(places, width + LANES), shrink_factors, expand_factors)
    returned = lax.all_to_all(
        terms.reshape(holders, capacity, columns), "wide", split_axis=0, concat_axis=0, tiled=True
    )
    return add_terms(base, returned.reshape(places, columns), chosen)


def solution(mesh):
    placed = (
        P(("parts", "wide"), None),
        P("wide", None),
        P(),
        P(None, ("parts", "wide")),
        P(("parts", "wide"), None),
        P("parts"),
        P(("parts", "wide")),
    )
    return jax.shard_map(
        per_device,
        mesh=mesh,
        in_specs=placed,
        out_specs=P(("parts", "wide"), None),
        check_vma=False,
    )
```

```python
import functools

import jax
import jax.numpy as jnp
from jax import lax
from jax.experimental import pallas as pl
from jax.experimental.pallas import tpu as pltpu
from jax.sharding import PartitionSpec as P

ADAPTER_RANK = 16
LANES = 128
MOST_VMEM = 60 * 1024 * 1024
VMEM_LIMIT = 48 * 1024 * 1024
BASE_PRODUCT = 240 * 10**8
BASE_SUM = 20 * 10**9
F32 = jnp.float32
BF16 = jnp.bfloat16


def _in_team(wide, quarter):
    return wide // (2 * quarter) * quarter + wide % quarter


def _from_team(number, team, quarter):
    return number // quarter * (2 * quarter) + team * quarter + number % quarter


def _step(width):
    return 1280 if width % 1280 == 0 else width


def _row_places(slot_ref, adapter_ref, adapters_held, capacity):
    adapters = slot_ref.shape[1]
    rows = adapter_ref.shape[1]
    held_bits = adapters_held.bit_length() - 1
    slots = slot_ref[...]
    high = jnp.broadcast_to((slots >> 6).astype(F32).astype(BF16), (8, adapters))
    low = jnp.broadcast_to((slots & 63).astype(F32).astype(BF16), (8, adapters))
    picks = lax.broadcasted_iota(jnp.int32, (adapters, rows), 0) == adapter_ref[...]
    picks = picks.astype(F32).astype(BF16)
    slot_high = jnp.dot(high, picks, preferred_element_type=F32)
    slot_low = jnp.dot(low, picks, preferred_element_type=F32)
    slot = (slot_high * 64.0 + slot_low)[:1].astype(jnp.int32)
    holder = slot >> held_bits
    local = slot & (adapters_held - 1)
    across = jnp.broadcast_to(holder.astype(F32), (rows, rows))
    earlier = lax.broadcasted_iota(jnp.int32, (rows, rows), 0) < lax.broadcasted_iota(
        jnp.int32, (rows, rows), 1
    )
    same = jnp.where(earlier & (across.T == across), 1.0, 0.0)
    rank = jnp.sum(same, axis=0, keepdims=True).astype(jnp.int32)
    return holder * capacity + rank, local


def _pack_kernel(adapters_held, capacity, slot_ref, adapter_ref, tokens_ref, out_ref, chosen_ref):
    rows, width = tokens_ref.shape
    places = out_ref.shape[0]
    place, local = _row_places(slot_ref, adapter_ref, adapters_held, capacity)
    sits = lax.broadcasted_iota(jnp.int32, (places, rows), 0) == place
    labels = jnp.sum(
        jnp.where(sits, (local + 1).astype(F32), 0.0), axis=1, keepdims=True
    )
    chosen = sits.astype(F32).astype(BF16)
    chosen_ref[...] = sits.astype(F32).T.astype(BF16)
    step = 1280 if width % 1280 == 0 else width
    for start in range(0, width, step):
        out_ref[:, start : start + step] = jnp.dot(
            chosen, tokens_ref[:, start : start + step], preferred_element_type=F32
        ).astype(BF16)
    out_ref[:, width:] = jnp.broadcast_to(labels, (places, LANES)).astype(BF16)


def pack(slots, adapters, tokens, adapters_held, capacity, places):
    rows, width = tokens.shape
    return pl.pallas_call(
        functools.partial(_pack_kernel, adapters_held, capacity),
        out_shape=(
            jax.ShapeDtypeStruct((places, width + LANES), BF16),
            jax.ShapeDtypeStruct((rows, places), BF16),
        ),
        compiler_params=pltpu.CompilerParams(vmem_limit_bytes=VMEM_LIMIT),
        cost_estimate=pl.CostEstimate(
            flops=2 * places * rows * width,
            bytes_accessed=2 * (rows + places) * width,
            transcendentals=0,
        ),
        name="pack_rows",
    )(slots, adapters, tokens)


def _adapter_kernel(
    rows_ref, shrink_ref, expand_ref, out_ref, held_ref, down_ref, up_ref, terms_ref, came_sem, gone_sem
):
    places = held_ref.shape[0]
    width, ranks = down_ref.shape
    step = width // 8
    cuts = [pl.ds(start, step) for start in range(0, width, step)]
    last = pl.ds(width, LANES)
    moves = []
    for cut in cuts:
        moves.append((rows_ref.at[:, cut], held_ref.at[:, cut]))
        moves.append((shrink_ref.at[cut, :], down_ref.at[cut, :]))
    moves += [(rows_ref.at[:, last], held_ref.at[:, last]), (expand_ref, up_ref)]
    coming = [pltpu.make_async_copy(*move, came_sem.at[i]) for i, move in enumerate(moves)]
    for copy in coming:
        copy.start()
    total = jnp.zeros((places, ranks), F32)
    for i, cut in enumerate(cuts):
        coming[2 * i].wait()
        coming[2 * i + 1].wait()
        total += jnp.dot(held_ref[:, cut], down_ref[cut, :], preferred_element_type=F32)
    coming[-2].wait()
    owner = lax.broadcasted_iota(jnp.int32, (places, ranks), 1) // ADAPTER_RANK + 1
    keep = held_ref[:, width : width + 1].astype(F32) == owner.astype(F32)
    shrunk = jnp.where(keep, total, 0.0).astype(BF16)
    coming[-1].wait()
    columns = terms_ref.shape[1]
    step = 512 if columns % 512 == 0 else columns
    going = []
    for i, start in enumerate(range(0, columns, step)):
        cut = pl.ds(start, step)
        terms_ref[:, cut] = jnp.dot(shrunk, up_ref[:, cut], preferred_element_type=F32).astype(BF16)
        going.append(pltpu.make_async_copy(terms_ref.at[:, cut], out_ref.at[:, cut], gone_sem.at[i]))
        going[-1].start()
    for copy in going:
        copy.wait()


def adapter_terms(arrived, shrink, expand):
    places = arrived.shape[0]
    width, ranks = shrink.shape
    columns = expand.shape[1]
    hbm = pl.BlockSpec(memory_space=pl.ANY)
    return pl.pallas_call(
        _adapter_kernel,
        in_specs=[hbm] * 3,
        out_specs=hbm,
        out_shape=jax.ShapeDtypeStruct((places, columns), BF16),
        scratch_shapes=[
            pltpu.VMEM(arrived.shape, BF16),
            pltpu.VMEM(shrink.shape, BF16),
            pltpu.VMEM(expand.shape, BF16),
            pltpu.VMEM((places, columns), BF16),
            pltpu.SemaphoreType.DMA((2 * 8 + 2,)),
            pltpu.SemaphoreType.DMA((pl.cdiv(columns, 512),)),
        ],
        compiler_params=pltpu.CompilerParams(vmem_limit_bytes=60 * 1024 * 1024),
        cost_estimate=pl.CostEstimate(
            flops=2 * places * ranks * (width + columns),
            bytes_accessed=2 * (places + ranks) * (width + columns),
            transcendentals=0,
        ),
        name="adapter_terms",
    )(arrived, shrink, expand)


def swap(x, axis, bit):
    size = lax.axis_size(axis)
    return lax.ppermute(x, axis, [(i, i ^ bit) for i in range(size)])


def gather_weights(weights, quarter, came):
    half = weights.shape[0] // 2
    mine = lax.axis_index("parts") * half
    own = lax.dynamic_slice_in_dim(weights, mine, half, 0)

    def across(x, axis, bit):
        return swap(x, axis, _from_team(bit, 0, quarter) if axis == "wide" else bit)

    upper, lower = quarter, quarter // 2
    far = across(own, "wide", upper)
    near = across(own, "wide", lower)
    near_x = [across(x, "parts", 1) for x in (own, near)]
    held = jnp.concatenate([own, near] + near_x, axis=0)
    far, *_ = lax.optimization_barrier((far, near))
    far = jnp.concatenate([far, across(far, "wide", lower)], axis=0)
    far, *_ = lax.optimization_barrier((far, came, *near_x))
    far = jnp.concatenate([far, across(far, "parts", 1)], axis=0)
    pieces = []
    for x, bit in ((held, 0), (far, upper)):
        known = [(bit ^ w, p) for p in (0, 1) for w in (0, lower)]
        pieces += [(x, known), (across(x, "wide", 1), [(w ^ 1, p) for w, p in known])]
    return pieces


def _base_kernel(marks, me_ref, *refs):
    count = len(marks)
    pieces = refs[:count]
    tokens_ref, came_ref, bias_ref, own_ref, other_ref, held_ref, left_ref = refs[count:]
    team, inside, parts = me_ref[0], me_ref[1], me_ref[2]
    rows = held_ref.shape[1]
    for piece, known in zip(pieces, marks, strict=True):
        for i, (w, p) in enumerate(known):
            held_ref[(inside ^ w) * 2 + (parts ^ p)] = piece[i * rows : (i + 1) * rows, :]
    own_rows, width = came_ref.shape
    columns = own_ref.shape[1]
    depth = width // 2
    for upper in (0, 1):
        block = pl.ds(pl.multiple_of((2 * upper + team) * depth, LANES), depth)
        left_ref[:own_rows, upper * depth : (upper + 1) * depth] = tokens_ref[:, block]
    left_ref[own_rows:, :] = came_ref[...]
    step = 256 if columns % 256 == 0 else columns

    for start in range(0, columns, step):
        block = held_ref[:, :, start : start + step].reshape(width, step)
        product = jnp.dot(left_ref[...], block, preferred_element_type=F32)
        own_ref[:, start : start + step] = product[:own_rows] + bias_ref[:, start : start + step].astype(F32)
        other_ref[:, start : start + step] = product[own_rows:].astype(BF16)


def base_product(me, tokens, came, bias, pieces, rows):
    marks = [known for _, known in pieces]
    columns = pieces[0][0].shape[1]
    own_rows, width = came.shape
    vmem = pl.BlockSpec(memory_space=pltpu.VMEM)
    return pl.pallas_call(
        functools.partial(_base_kernel, marks),
        in_specs=[pl.BlockSpec(memory_space=pltpu.SMEM)] + [vmem] * (len(pieces) + 3),
        out_specs=(vmem, vmem),
        out_shape=(
            jax.ShapeDtypeStruct((own_rows, columns), F32),
            jax.ShapeDtypeStruct((own_rows, columns), BF16),
        ),
        scratch_shapes=[
            pltpu.VMEM((width // rows, rows, columns), BF16),
            pltpu.VMEM((2 * own_rows, width), BF16),
        ],
        compiler_params=pltpu.CompilerParams(vmem_limit_bytes=VMEM_LIMIT),
        cost_estimate=pl.CostEstimate(
            flops=BASE_PRODUCT,
            bytes_accessed=2 * width * columns,
            transcendentals=0,
        ),
        name="base_product",
    )(me, *[x for x, _ in pieces], tokens, came, bias)


def _base_sum_kernel(own_ref, other_ref, out_ref):
    out_ref[...] = own_ref[...] + other_ref[...].astype(F32)


def base_sum(own, other):
    return pl.pallas_call(
        _base_sum_kernel,
        out_shape=jax.ShapeDtypeStruct(own.shape, F32),
        compiler_params=pltpu.CompilerParams(vmem_limit_bytes=VMEM_LIMIT),
        cost_estimate=pl.CostEstimate(flops=BASE_SUM, bytes_accessed=10 * own.size, transcendentals=0),
        name="base_sum",
    )(own, other)


def _add_terms_kernel(base_ref, returned_ref, chosen_ref, out_ref):
    terms = jnp.dot(chosen_ref[...], returned_ref[...], preferred_element_type=F32)
    out_ref[...] = (base_ref[...] + 2.0 * terms).astype(BF16)


def add_terms(base, returned, chosen):
    return pl.pallas_call(
        _add_terms_kernel,
        out_shape=jax.ShapeDtypeStruct(base.shape, BF16),
        compiler_params=pltpu.CompilerParams(vmem_limit_bytes=VMEM_LIMIT),
        name="add_terms",
    )(base, returned, chosen)


def per_device(
    tokens,
    key_weight_matrix,
    key_bias_vector,
    shrink_factors,
    expand_factors,
    adapter_slot_index,
    row_adapter_index,
):
    rows, width = tokens.shape
    holders = lax.axis_size("wide")
    capacity = 2 * rows // holders
    places = holders * capacity
    adapters_held = expand_factors.shape[0] // ADAPTER_RANK
    columns = expand_factors.shape[1]

    slots, adapters, bias = adapter_slot_index[None, :], row_adapter_index[None, :], key_bias_vector[None, :]
    outgoing, chosen = pack(slots, adapters, tokens, adapters_held, capacity, places)
    arrived = lax.all_to_all(
        outgoing.reshape(holders, capacity, width + LANES), "wide", split_axis=0, concat_axis=0, tiled=True
    )
    half = key_weight_matrix.shape[0] // 2
    if holders == 16 and half % 16 == 0 and width % (4 * LANES) == 0:
        quarter, depth = holders // 4, width // 4
        wide, parts = lax.axis_index("wide"), lax.axis_index("parts")
        team = wide // quarter % 2
        far = [lax.dynamic_slice_in_dim(tokens, (2 * upper + 1 - team) * depth, depth, 1) for upper in (0, 1)]
        came = swap(jnp.concatenate(far, axis=1), "wide", quarter)
        pieces = gather_weights(key_weight_matrix, quarter, came)
        me = jnp.stack([team, _in_team(wide, quarter), parts]).astype(jnp.int32)
        own, other = base_product(me, tokens, came, bias, pieces, half)
        arrived, _ = lax.optimization_barrier((arrived, other))
        base = base_sum(own, swap(other, "wide", quarter))
    else:
        gathered = lax.all_gather(key_weight_matrix, "wide", axis=0, tiled=True)
        base = jnp.dot(tokens, gathered, preferred_element_type=F32) + bias.astype(F32)
    terms = adapter_terms(arrived.reshape(places, width + LANES), shrink_factors, expand_factors)
    returned = lax.all_to_all(
        terms.reshape(holders, capacity, columns), "wide", split_axis=0, concat_axis=0, tiled=True
    )
    return add_terms(base, returned.reshape(places, columns), chosen)


def solution(mesh):
    placed = (
        P(("parts", "wide"), None),
        P("wide", None),
        P(),
        P(None, ("parts", "wide")),
        P(("parts", "wide"), None),
        P("parts"),
        P(("parts", "wide")),
    )
    return jax.shard_map(
        per_device,
        mesh=mesh,
        in_specs=placed,
        out_specs=P(("parts", "wide"), None),
        check_vma=False,
    )
```

```python
import functools

import jax
import jax.numpy as jnp
from jax import lax
from jax.experimental import pallas as pl
from jax.experimental.pallas import tpu as pltpu
from jax.sharding import PartitionSpec as P

ADAPTER_RANK = 16
LANES = 128
MOST_VMEM = 60 * 1024 * 1024
VMEM_LIMIT = 48 * 1024 * 1024
BASE_PRODUCT = 240 * 10**8
BASE_SUM = 20 * 10**9
F32 = jnp.float32
BF16 = jnp.bfloat16


def _in_team(wide, quarter):
    return wide // (2 * quarter) * quarter + wide % quarter


def _from_team(number, team, quarter):
    return number // quarter * (2 * quarter) + team * quarter + number % quarter


def _step(width):
    return 1280 if width % 1280 == 0 else width


def _row_places(slot_ref, adapter_ref, adapters_held, capacity):
    adapters = slot_ref.shape[1]
    rows = adapter_ref.shape[1]
    held_bits = adapters_held.bit_length() - 1
    slots = slot_ref[...]
    high = jnp.broadcast_to((slots >> 6).astype(F32).astype(BF16), (8, adapters))
    low = jnp.broadcast_to((slots & 63).astype(F32).astype(BF16), (8, adapters))
    picks = lax.broadcasted_iota(jnp.int32, (adapters, rows), 0) == adapter_ref[...]
    picks = picks.astype(F32).astype(BF16)
    slot_high = jnp.dot(high, picks, preferred_element_type=F32)
    slot_low = jnp.dot(low, picks, preferred_element_type=F32)
    slot = (slot_high * 64.0 + slot_low)[:1].astype(jnp.int32)
    holder = slot >> held_bits
    local = slot & (adapters_held - 1)
    across = jnp.broadcast_to(holder.astype(F32), (rows, rows))
    earlier = lax.broadcasted_iota(jnp.int32, (rows, rows), 0) < lax.broadcasted_iota(
        jnp.int32, (rows, rows), 1
    )
    same = jnp.where(earlier & (across.T == across), 1.0, 0.0)
    rank = jnp.sum(same, axis=0, keepdims=True).astype(jnp.int32)
    return holder * capacity + rank, local


def _pack_kernel(adapters_held, capacity, slot_ref, adapter_ref, tokens_ref, out_ref, chosen_ref):
    rows, width = tokens_ref.shape
    places = out_ref.shape[0]
    place, local = _row_places(slot_ref, adapter_ref, adapters_held, capacity)
    sits = lax.broadcasted_iota(jnp.int32, (places, rows), 0) == place
    labels = jnp.sum(
        jnp.where(sits, (local + 1).astype(F32), 0.0), axis=1, keepdims=True
    )
    chosen = sits.astype(F32).astype(BF16)
    chosen_ref[...] = sits.astype(F32).T.astype(BF16)
    step = 1280 if width % 1280 == 0 else width
    for start in range(0, width, step):
        out_ref[:, start : start + step] = jnp.dot(
            chosen, tokens_ref[:, start : start + step], preferred_element_type=F32
        ).astype(BF16)
    out_ref[:, width:] = jnp.broadcast_to(labels, (places, LANES)).astype(BF16)


def pack(slots, adapters, tokens, adapters_held, capacity, places):
    rows, width = tokens.shape
    return pl.pallas_call(
        functools.partial(_pack_kernel, adapters_held, capacity),
        out_shape=(
            jax.ShapeDtypeStruct((places, width + LANES), BF16),
            jax.ShapeDtypeStruct((rows, places), BF16),
        ),
        compiler_params=pltpu.CompilerParams(vmem_limit_bytes=VMEM_LIMIT),
        cost_estimate=pl.CostEstimate(
            flops=2 * places * rows * width,
            bytes_accessed=2 * (rows + places) * width,
            transcendentals=0,
        ),
        name="pack_rows",
    )(slots, adapters, tokens)


def _adapter_kernel(
    rows_ref, shrink_ref, expand_ref, out_ref, held_ref, down_ref, up_ref, terms_ref, came_sem, gone_sem
):
    places = held_ref.shape[0]
    width, ranks = down_ref.shape
    step = width // 8
    cuts = [pl.ds(start, step) for start in range(0, width, step)]
    last = pl.ds(width, LANES)
    moves = []
    for cut in cuts:
        moves.append((rows_ref.at[:, cut], held_ref.at[:, cut]))
        moves.append((shrink_ref.at[cut, :], down_ref.at[cut, :]))
    moves += [(rows_ref.at[:, last], held_ref.at[:, last]), (expand_ref, up_ref)]
    coming = [pltpu.make_async_copy(*move, came_sem.at[i]) for i, move in enumerate(moves)]
    for copy in coming:
        copy.start()
    total = jnp.zeros((places, ranks), F32)
    for i, cut in enumerate(cuts):
        coming[2 * i].wait()
        coming[2 * i + 1].wait()
        total += jnp.dot(held_ref[:, cut], down_ref[cut, :], preferred_element_type=F32)
    coming[-2].wait()
    owner = lax.broadcasted_iota(jnp.int32, (places, ranks), 1) // ADAPTER_RANK + 1
    keep = held_ref[:, width : width + 1].astype(F32) == owner.astype(F32)
    shrunk = jnp.where(keep, total, 0.0).astype(BF16)
    coming[-1].wait()
    columns = terms_ref.shape[1]
    step = 256 if columns % 256 == 0 else columns
    going = []
    for i, start in enumerate(range(0, columns, step)):
        cut = pl.ds(start, step)
        terms_ref[:, cut] = jnp.dot(shrunk, up_ref[:, cut], preferred_element_type=F32).astype(BF16)
        going.append(pltpu.make_async_copy(terms_ref.at[:, cut], out_ref.at[:, cut], gone_sem.at[i]))
        going[-1].start()
    for copy in going:
        copy.wait()


def adapter_terms(arrived, shrink, expand):
    places = arrived.shape[0]
    width, ranks = shrink.shape
    columns = expand.shape[1]
    hbm = pl.BlockSpec(memory_space=pl.ANY)
    return pl.pallas_call(
        _adapter_kernel,
        in_specs=[hbm] * 3,
        out_specs=hbm,
        out_shape=jax.ShapeDtypeStruct((places, columns), BF16),
        scratch_shapes=[
            pltpu.VMEM(arrived.shape, BF16),
            pltpu.VMEM(shrink.shape, BF16),
            pltpu.VMEM(expand.shape, BF16),
            pltpu.VMEM((places, columns), BF16),
            pltpu.SemaphoreType.DMA((2 * 8 + 2,)),
            pltpu.SemaphoreType.DMA((pl.cdiv(columns, 256),)),
        ],
        compiler_params=pltpu.CompilerParams(vmem_limit_bytes=60 * 1024 * 1024),
        cost_estimate=pl.CostEstimate(
            flops=2 * places * ranks * (width + columns),
            bytes_accessed=2 * (places + ranks) * (width + columns),
            transcendentals=0,
        ),
        name="adapter_terms",
    )(arrived, shrink, expand)


def swap(x, axis, bit):
    size = lax.axis_size(axis)
    return lax.ppermute(x, axis, [(i, i ^ bit) for i in range(size)])


def gather_weights(weights, quarter, came):
    half = weights.shape[0] // 2
    mine = lax.axis_index("parts") * half
    own = lax.dynamic_slice_in_dim(weights, mine, half, 0)

    def across(x, axis, bit):
        return swap(x, axis, _from_team(bit, 0, quarter) if axis == "wide" else bit)

    upper, lower = quarter, quarter // 2
    far = across(own, "wide", upper)
    near = across(own, "wide", lower)
    near_x = [across(x, "parts", 1) for x in (own, near)]
    held = jnp.concatenate([own, near] + near_x, axis=0)
    far, *_ = lax.optimization_barrier((far, near))
    far = jnp.concatenate([far, across(far, "wide", lower)], axis=0)
    far, *_ = lax.optimization_barrier((far, came, *near_x))
    far = jnp.concatenate([far, across(far, "parts", 1)], axis=0)
    pieces = []
    for x, bit in ((held, 0), (far, upper)):
        known = [(bit ^ w, p) for p in (0, 1) for w in (0, lower)]
        pieces += [(x, known), (across(x, "wide", 1), [(w ^ 1, p) for w, p in known])]
    return pieces


def _base_kernel(marks, me_ref, *refs):
    count = len(marks)
    pieces = refs[:count]
    tokens_ref, came_ref, bias_ref, own_ref, other_ref, held_ref, left_ref = refs[count:]
    team, inside, parts = me_ref[0], me_ref[1], me_ref[2]
    rows = held_ref.shape[1]
    for piece, known in zip(pieces, marks, strict=True):
        for i, (w, p) in enumerate(known):
            held_ref[(inside ^ w) * 2 + (parts ^ p)] = piece[i * rows : (i + 1) * rows, :]
    own_rows, width = came_ref.shape
    columns = own_ref.shape[1]
    depth = width // 2
    for upper in (0, 1):
        block = pl.ds(pl.multiple_of((2 * upper + team) * depth, LANES), depth)
        left_ref[:own_rows, upper * depth : (upper + 1) * depth] = tokens_ref[:, block]
    left_ref[own_rows:, :] = came_ref[...]
    step = 256 if columns % 256 == 0 else columns

    for start in range(0, columns, step):
        block = held_ref[:, :, start : start + step].reshape(width, step)
        product = jnp.dot(left_ref[...], block, preferred_element_type=F32)
        own_ref[:, start : start + step] = product[:own_rows] + bias_ref[:, start : start + step].astype(F32)
        other_ref[:, start : start + step] = product[own_rows:].astype(BF16)


def base_product(me, tokens, came, bias, pieces, rows):
    marks = [known for _, known in pieces]
    columns = pieces[0][0].shape[1]
    own_rows, width = came.shape
    vmem = pl.BlockSpec(memory_space=pltpu.VMEM)
    return pl.pallas_call(
        functools.partial(_base_kernel, marks),
        in_specs=[pl.BlockSpec(memory_space=pltpu.SMEM)] + [vmem] * (len(pieces) + 3),
        out_specs=(vmem, vmem),
        out_shape=(
            jax.ShapeDtypeStruct((own_rows, columns), F32),
            jax.ShapeDtypeStruct((own_rows, columns), BF16),
        ),
        scratch_shapes=[
            pltpu.VMEM((width // rows, rows, columns), BF16),
            pltpu.VMEM((2 * own_rows, width), BF16),
        ],
        compiler_params=pltpu.CompilerParams(vmem_limit_bytes=VMEM_LIMIT),
        cost_estimate=pl.CostEstimate(
            flops=BASE_PRODUCT,
            bytes_accessed=2 * width * columns,
            transcendentals=0,
        ),
        name="base_product",
    )(me, *[x for x, _ in pieces], tokens, came, bias)


def _base_sum_kernel(own_ref, other_ref, out_ref):
    out_ref[...] = own_ref[...] + other_ref[...].astype(F32)


def base_sum(own, other):
    return pl.pallas_call(
        _base_sum_kernel,
        out_shape=jax.ShapeDtypeStruct(own.shape, F32),
        compiler_params=pltpu.CompilerParams(vmem_limit_bytes=VMEM_LIMIT),
        cost_estimate=pl.CostEstimate(flops=BASE_SUM, bytes_accessed=10 * own.size, transcendentals=0),
        name="base_sum",
    )(own, other)


def _add_terms_kernel(base_ref, returned_ref, chosen_ref, out_ref):
    terms = jnp.dot(chosen_ref[...], returned_ref[...], preferred_element_type=F32)
    out_ref[...] = (base_ref[...] + 2.0 * terms).astype(BF16)


def add_terms(base, returned, chosen):
    return pl.pallas_call(
        _add_terms_kernel,
        out_shape=jax.ShapeDtypeStruct(base.shape, BF16),
        compiler_params=pltpu.CompilerParams(vmem_limit_bytes=VMEM_LIMIT),
        name="add_terms",
    )(base, returned, chosen)


def per_device(
    tokens,
    key_weight_matrix,
    key_bias_vector,
    shrink_factors,
    expand_factors,
    adapter_slot_index,
    row_adapter_index,
):
    rows, width = tokens.shape
    holders = lax.axis_size("wide")
    capacity = 2 * rows // holders
    places = holders * capacity
    adapters_held = expand_factors.shape[0] // ADAPTER_RANK
    columns = expand_factors.shape[1]

    slots, adapters, bias = adapter_slot_index[None, :], row_adapter_index[None, :], key_bias_vector[None, :]
    outgoing, chosen = pack(slots, adapters, tokens, adapters_held, capacity, places)
    arrived = lax.all_to_all(
        outgoing.reshape(holders, capacity, width + LANES), "wide", split_axis=0, concat_axis=0, tiled=True
    )
    half = key_weight_matrix.shape[0] // 2
    if holders == 16 and half % 16 == 0 and width % (4 * LANES) == 0:
        quarter, depth = holders // 4, width // 4
        wide, parts = lax.axis_index("wide"), lax.axis_index("parts")
        team = wide // quarter % 2
        far = [lax.dynamic_slice_in_dim(tokens, (2 * upper + 1 - team) * depth, depth, 1) for upper in (0, 1)]
        came = swap(jnp.concatenate(far, axis=1), "wide", quarter)
        pieces = gather_weights(key_weight_matrix, quarter, came)
        me = jnp.stack([team, _in_team(wide, quarter), parts]).astype(jnp.int32)
        own, other = base_product(me, tokens, came, bias, pieces, half)
        arrived, _ = lax.optimization_barrier((arrived, other))
        base = base_sum(own, swap(other, "wide", quarter))
    else:
        gathered = lax.all_gather(key_weight_matrix, "wide", axis=0, tiled=True)
        base = jnp.dot(tokens, gathered, preferred_element_type=F32) + bias.astype(F32)
    terms = adapter_terms(arrived.reshape(places, width + LANES), shrink_factors, expand_factors)
    returned = lax.all_to_all(
        terms.reshape(holders, capacity, columns), "wide", split_axis=0, concat_axis=0, tiled=True
    )
    return add_terms(base, returned.reshape(places, columns), chosen)


def solution(mesh):
    placed = (
        P(("parts", "wide"), None),
        P("wide", None),
        P(),
        P(None, ("parts", "wide")),
        P(("parts", "wide"), None),
        P("parts"),
        P(("parts", "wide")),
    )
    return jax.shard_map(
        per_device,
        mesh=mesh,
        in_specs=placed,
        out_specs=P(("parts", "wide"), None),
        check_vma=False,
    )
```
